32 devices in a mesh: rig: 2 (over y), row: 4 (over z), col: 4 (over x, core).
Axes of the slice: x: 2, y: 2, z: 4, core: 2. Of those that a mesh axis runs over, the one named last changes fastest.
Arguments:
- jacobian: bfloat16 [8, 4, 64, 64, 1024], P(('rig', 'row'), 'col'), parts along dimension 0, may hold values from -0.375 to 0.375
- block_rows: int32 [8, 4, 1024], P(('rig', 'row'), 'col'), parts along dimension 0, may hold values from 0 to 511
- block_cols: int32 [8, 4, 1024], P(('rig', 'row'), 'col'), parts along dimension 0, may hold values from 0 to 511
- counts: int32 [8, 4], P(('rig', 'row'), 'col'), parts along dimension 0, may hold values from 128 to 1024, as said below
- residuals: float32 [64, 4096], P(None, ('rig', 'row')), parts along dimension 1, may hold values from -6 to 6
- damping: float32 [64, 4096], P(None, ('rig', 'col')), parts along dimension 1, may hold values from 0.5 to 2
Outputs:
- step_field: float32 [64, 4096], P(None, ('rig', 'col')), parts along dimension 1
- normal_residual: float32 [64, 4096], P(None, ('rig', 'col')), parts along dimension 1
The draws below stay inside these ranges and needn't reach their ends.
There are 2 independent parts, one for each index of `rig`. The reference program is written for one: setup_inputs(seed, part) draws one part's arguments, and reference() takes and returns one part's arrays. A program takes and returns all parts, laid end to end along the dimension named above; each array names one. Nothing has to cross between parts.
Inputs may be any that keep to these rules, and one draw needn't show every extreme that they name: `counts`: live slots of one cell; 1024 is reached on some cell and 128 on another in every draw.
All inputs are finite; a program needn't handle non-finite values.
Results may differ from the reference program's by a relative error of at most 0.0003.
Values sent between devices are 32-bit elements; how exact they have to be, the bound alone decides.
A program may use at most 64 MiB of HBM per device.

```python
import math
import jax
import jax.numpy as jnp
from jax import lax

B = 64
RB_DEV = 512
CB_DEV = 512
CAP = 1024
ITERS = 2
NRB = 2048
NCB = 2048
N_ROW = 4
N_COL = 4


def draw_counts(key, part):
    key = jax.random.fold_in(key, 11)
    first, second, third = jax.random.split(key, 3)
    cells = N_ROW * N_COL
    values = jax.random.randint(first, (cells,), CAP // 8, CAP + 1)
    top_spot = jax.random.randint(second, (), 0, cells)
    low_spot = (top_spot + 1 + jax.random.randint(third, (), 0, cells - 1)) % cells
    positions = jnp.arange(cells)
    values = jnp.where(positions == top_spot, CAP, values)
    values = jnp.where(positions == low_spot, CAP // 8, values)
    return values.reshape(N_ROW, N_COL).astype(jnp.int32)


def set_ends(entries, rng, least, largest):
    spot = [jax.random.randint(jax.random.fold_in(rng, axis), (), 0, length) for axis, length in enumerate(entries.shape)]
    main_axis = entries.shape.index(max(entries.shape))
    beside = spot[:main_axis] + [(spot[main_axis] + 1) % entries.shape[main_axis]] + spot[main_axis + 1:]
    return entries.at[tuple(spot)].set(least).at[tuple(beside)].set(largest)


def levels(key, extent, cuts, least, largest):
    loudness, own = 1.0, jax.random.fold_in(key, 6)
    for position, shards_of in cuts:
        steps = jnp.exp(jax.random.uniform(jax.random.fold_in(own, position), (shards_of,), jnp.float32, least / len(cuts), largest / len(cuts)))
        loudness = loudness * jnp.repeat(steps, extent[position] // shards_of).reshape([-1 if axis == position else 1 for axis in range(len(extent))])
    return loudness


def normal_values(stream_key, extent, deviation, most, cuts=(), kind=jnp.bfloat16):
    array = deviation * jax.random.normal(stream_key, extent, jnp.float32)
    if cuts:
        array = array * levels(stream_key, extent, cuts, -0.22, 0.18)
    return jnp.clip(array, -most, most).astype(kind)


def setup_inputs(seed: int = 0, part: int = 0) -> dict:
    keys = jax.random.split(jax.random.key(seed), 7)
    part_keys = jax.random.split(jax.random.fold_in(keys[6], part), 7)
    return {
        "jacobian": normal_values(part_keys[0], (N_ROW, N_COL, B, B, CAP), (4 * B) ** -0.5, 0.375, ((0, 4), (1, 4))),
        "block_rows": set_ends(jax.random.randint(part_keys[1], (N_ROW, N_COL, CAP), 0, RB_DEV), jax.random.fold_in(part_keys[1], 1), 0, RB_DEV - 1).astype(jnp.int32),
        "block_cols": set_ends(jax.random.randint(part_keys[2], (N_ROW, N_COL, CAP), 0, CB_DEV), jax.random.fold_in(part_keys[2], 1), 0, CB_DEV - 1).astype(jnp.int32),
        "counts": draw_counts(jax.random.fold_in(jax.random.fold_in(keys[6], part), 71), part),
        "residuals": normal_values(part_keys[4], (B, NRB), 1.0, 6.0, ((1, 4),), jnp.float32),
        "damping": jnp.clip(jnp.exp(math.log(2.0) - 1.3862944 * jax.random.uniform(part_keys[5], (B, NCB), jnp.float32) ** levels(part_keys[5], (B, NCB), ((1, 4),), -0.2, 0.2)), 0.5, 2.0),
    }


def spread(terms, index, width):
    onehot = (index[:, None] == jnp.arange(width, dtype=jnp.int32)[None, :]).astype(jnp.float32)
    return jnp.dot(terms, onehot, precision=lax.Precision.HIGHEST)


def forward(jacobian, block_rows, block_cols, counts, vector):
    pieces = vector.reshape(B, N_COL, CB_DEV)
    slots = jnp.arange(CAP, dtype=jnp.int32)

    def one_row(i):
        def one_cell(j):
            source = pieces[:, j, :]
            gathered = jnp.take(source, block_cols[i, j], axis=1)
            live = (slots < counts[i, j]).astype(jnp.float32)
            terms = jnp.sum(jacobian[i, j].astype(jnp.float32) * gathered[None, :, :], axis=1) * live
            return spread(terms, block_rows[i, j], RB_DEV)
        return jnp.sum(lax.map(one_cell, jnp.arange(N_COL, dtype=jnp.int32)), axis=0)

    result = lax.map(one_row, jnp.arange(N_ROW, dtype=jnp.int32))
    return jnp.transpose(result, (1, 0, 2)).reshape(B, N_ROW * RB_DEV)


def backward(jacobian, block_rows, block_cols, counts, vector):
    pieces = vector.reshape(B, N_ROW, RB_DEV)
    slots = jnp.arange(CAP, dtype=jnp.int32)

    def one_col(j):
        def one_cell(i):
            source = pieces[:, i, :]
            gathered = jnp.take(source, block_rows[i, j], axis=1)
            live = (slots < counts[i, j]).astype(jnp.float32)
            terms = jnp.sum(jacobian[i, j].astype(jnp.float32) * gathered[:, None, :], axis=0) * live
            return spread(terms, block_cols[i, j], CB_DEV)
        return jnp.sum(lax.map(one_cell, jnp.arange(N_ROW, dtype=jnp.int32)), axis=0)

    result = lax.map(one_col, jnp.arange(N_COL, dtype=jnp.int32))
    return jnp.transpose(result, (1, 0, 2)).reshape(B, N_COL * CB_DEV)


def reference(jacobian, block_rows, block_cols, counts, residuals, damping):
    rhs = -backward(jacobian, block_rows, block_cols, counts, residuals)
    step_field = jnp.zeros_like(rhs)
    normal_residual = rhs
    direction = rhs
    norm_now = jnp.sum(normal_residual * normal_residual)
    for step in range(ITERS):
        image = forward(jacobian, block_rows, block_cols, counts, direction)
        curv = jnp.sum(image * image) + jnp.sum(direction * damping * direction)
        alpha = norm_now / curv
        step_field = step_field + alpha * direction
        pulled = backward(jacobian, block_rows, block_cols, counts, image) + damping * direction
        normal_residual = normal_residual - alpha * pulled
        norm_next = jnp.sum(normal_residual * normal_residual)
        direction = normal_residual + (norm_next / norm_now) * direction
        norm_now = norm_next
    return step_field, normal_residual
```

```python
import functools

import jax
import jax.numpy as jnp
from jax import lax
from jax.experimental import pallas as pl
from jax.experimental.pallas import tpu as pltpu
from jax.sharding import PartitionSpec as P

F32 = jnp.float32
BF16 = jnp.bfloat16
MESH = pl.DeviceIdType.MESH
LANES = 128
SUB = 8
LOADS = 4


class Group:
    def __init__(self, axis, size, rows):
        self.axis = axis
        self.n = size
        self.owners = min(size, 4)
        self.step = size // self.owners
        self.rows = rows // self.owners

    def locate(self):
        self.me = lax.axis_index(self.axis)
        self.mine = self.me // self.step

    def chunk(self, d):
        if d == 0:
            return self.mine
        if self.owners == 4:
            if d == 1:
                return self.mine + 1 - 2 * lax.rem(self.mine, 2)
            if d == 2:
                return lax.rem(self.mine + 2, 4)
            return 3 - self.mine
        return lax.rem(self.mine + d, self.owners)

    def peer(self, d):
        if self.n == self.owners:
            return self.chunk(d)
        return lax.rem(self.me + d, self.n)

    def when_owner(self, action):
        if self.step == 1:
            action()
        else:
            pl.when(lax.rem(self.me, self.step) == 0)(action)

    def when_not_owner(self, action):
        if self.step > 1:
            pl.when(lax.rem(self.me, self.step) != 0)(action)


class Sum:
    def __init__(self, group, k, part, recv, full, sems):
        self.g, self.k = group, k
        self.part, self.recv, self.full = part, recv, full
        self.rs_send, self.rs_recv, self.ag_send, self.ag_recv = sems

    def rs(self, c, src, target):
        return pltpu.make_async_remote_copy(
            src_ref=self.part.at[self.k, c],
            dst_ref=self.recv.at[self.k, src],
            send_sem=self.rs_send.at[self.k, c],
            recv_sem=self.rs_recv.at[self.k, src],
            device_id={self.g.axis: target},
            device_id_type=MESH,
        )

    def ag(self, c, target):
        return pltpu.make_async_remote_copy(
            src_ref=self.full.at[self.k, c],
            dst_ref=self.full.at[self.k, c],
            send_sem=self.ag_send.at[self.k, target],
            recv_sem=self.ag_recv.at[self.k, c],
            device_id={self.g.axis: target},
            device_id_type=MESH,
        )

    def scatter(self):
        g = self.g
        for d in reversed(range(g.owners)):
            c = g.chunk(d)
            if d == 0:
                g.when_not_owner(lambda: self.rs(g.mine, g.me, g.mine * g.step).start())
            else:
                self.rs(c, g.me, c * g.step).start()

    def reduce(self):
        g = self.g

        def own():
            total = self.part[self.k, g.mine]
            for d in range(1, g.n):
                src = g.peer(d)
                self.rs(g.mine, src, g.me).wait_recv()
                total = total + self.recv[self.k, src]
            self.full[self.k, g.mine] = total
            for d in reversed(range(1, g.n)):
                self.ag(g.mine, g.peer(d)).start()

        g.when_owner(own)

    def arrive(self, d):
        g = self.g
        c = g.chunk(d)
        if d == 0:
            g.when_not_owner(lambda: self.ag(c, g.me).wait_recv())
        else:
            self.ag(c, g.me).wait_recv()
        return c

    def drain(self):
        g = self.g
        for d in range(g.owners):
            c = g.chunk(d)
            if d == 0:
                g.when_not_owner(lambda: self.rs(g.mine, g.me, g.mine * g.step).wait_send())
            else:
                self.rs(c, g.me, c * g.step).wait_send()

        def own():
            for d in range(1, g.n):
                self.ag(g.mine, g.peer(d)).wait_send()

        g.when_owner(own)


class Tile:
    def __init__(self, group, k, buf, send, recv):
        self.g, self.k, self.buf, self.send, self.recv = group, k, buf, send, recv

    def copy(self, slot, target):
        return pltpu.make_async_remote_copy(
            src_ref=self.buf.at[self.k, slot],
            dst_ref=self.buf.at[self.k, slot],
            send_sem=self.send.at[self.k, target],
            recv_sem=self.recv.at[self.k, slot],
            device_id={self.g.axis: target},
            device_id_type=MESH,
        )

    def start(self, value):
        g = self.g
        self.buf[self.k, g.me] = value
        for d in range(1, g.n):
            self.copy(g.me, g.peer(d)).start()

    def total(self):
        g = self.g
        for d in range(1, g.n):
            self.copy(g.peer(d), g.me).wait_recv()
        total = self.buf[self.k, 0]
        for slot in range(1, g.n):
            total = total + self.buf[self.k, slot]
        return total

    def drain(self):
        for d in range(1, self.g.n):
            self.copy(self.g.me, self.g.peer(d)).wait_send()


def pieces(x):
    high = x.astype(BF16)
    low = (x - high.astype(F32)).astype(BF16)
    return jnp.concatenate([high, low], axis=0)


def fold(x):
    total = None
    for r in range(0, x.shape[0], SUB):
        for c in range(0, x.shape[1], LANES):
            block = x[r : r + SUB, c : c + LANES]
            total = block if total is None else total + block
    return total


def whole(tile):
    return jnp.sum(tile, axis=(0, 1), keepdims=True)


def kernel(
    row, col, jac_hbm, rows_ref, cols_ref, count_ref, res_ref, damp_ref, step_ref, out_ref,
    jac, oh_r, oh_c, g_ref, terms, acc3, r1_ref,
    part_r, recv_r, full_r, part_c, recv_c, full_c, tiles,
    load_sem, rs_send, rs_recv, ag_send, ag_recv, t_send, t_recv,
):
    entries, _, slots = jac.shape
    row.locate()
    col.locate()
    sems_r = (rs_send.at[0], rs_recv.at[0], ag_send.at[0], ag_recv.at[0])
    sems_c = (rs_send.at[1], rs_recv.at[1], ag_send.at[1], ag_recv.at[1])

    per = entries // LOADS

    def load(q):
        part = pl.ds(q * per, per)
        return pltpu.make_async_copy(jac_hbm.at[part], jac.at[part], load_sem.at[q])

    for q in range(LOADS):
        load(q).start()

    barrier = pltpu.get_barrier_semaphore()
    for g in (row, col):
        for d in range(1, g.n):
            pl.semaphore_signal(
                barrier, inc=1, device_id={g.axis: g.peer(d)}, device_id_type=MESH
            )

    live = lax.broadcasted_iota(jnp.int32, (1, slots), 1) < count_ref[0, 0]
    for idx_ref, oh in ((rows_ref, oh_r), (cols_ref, oh_c)):
        width = oh.shape[0]
        index = jnp.where(live, idx_ref[...], -1)
        step = 64

        def build(i, _, index=index, oh=oh, step=step):
            at = pl.multiple_of(i * step, step)
            ids = lax.broadcasted_iota(jnp.int32, (step, slots), 0) + at
            oh[pl.ds(at, step), :] = jnp.where(ids == index, 1.0, 0.0).astype(BF16)
            return 0

        lax.fori_loop(0, width // step, build, 0)

    def gather(x, oh):
        rows = x.shape[0]
        y = jnp.dot(pieces(x), oh[...], preferred_element_type=F32)
        g_ref[pl.ds(0, rows), :] = y[:rows] + y[rows:]

    def add_back(a0, rows, first):
        def body(kk, _):
            sl = pl.ds(pl.multiple_of(kk * LANES, LANES), LANES)
            acc = None if first else terms[:, sl]
            for a in range(rows):
                term = jac[a0 + a, :, sl].astype(F32) * g_ref[a : a + 1, sl]
                acc = term if acc is None else acc + term
            terms[:, sl] = acc
            return 0

        lax.fori_loop(0, slots // LANES, body, 0)

    def add_forth(b0, rows, first):
        b0 = pl.multiple_of(b0, rows)

        def body(kk, _):
            sl = pl.ds(pl.multiple_of(kk * LANES, LANES), LANES)
            g = g_ref[pl.ds(0, rows), sl]
            for a in range(entries):
                m = jac[a, pl.ds(b0, rows), sl].astype(F32) * g
                part = m[:SUB]
                for r in range(SUB, rows, SUB):
                    part = part + m[r : r + SUB]
                acc3[a, :, sl] = part if first else acc3[a, :, sl] + part
            return 0

        lax.fori_loop(0, slots // LANES, body, 0)

    def close_forth():
        def body(kk, _):
            sl = pl.ds(pl.multiple_of(kk * LANES, LANES), LANES)
            terms[:, sl] = jnp.sum(acc3[:, :, sl], axis=1)
            return 0

        lax.fori_loop(0, slots // LANES, body, 0)

    def spread(oh, s):
        y = lax.dot_general(
            pieces(terms[...]), oh[...], (((1,), (1,)), ((), ())), preferred_element_type=F32
        )
        out = y[:entries] + y[entries:]
        n = s.g.rows
        for c in range(s.g.owners):
            s.part[s.k, c] = out[c * n : (c + 1) * n]
        s.scatter()
        s.reduce()

    def sum_r(k):
        return Sum(row, k, part_r, recv_r, full_r, sems_r)

    def sum_c(k):
        return Sum(col, k, part_c, recv_c, full_c, sems_c)

    sums = [sum_r(0), sum_c(0), sum_r(1), sum_c(1), sum_r(2)]
    groups = (col, row, col, row, col)
    exchanges = [Tile(g, k, tiles, t_send, t_recv) for k, g in enumerate(groups)]
    nothing = jnp.zeros((SUB, LANES), F32)

    def pair(first, second=nothing):
        return jnp.concatenate([first, second], axis=0)

    def damp(c):
        return damp_ref[pl.ds(pl.multiple_of(c * row.rows, SUB), row.rows), :]

    def fold_all(group, value):
        total = value(0)
        for c in range(1, group.owners):
            total = total + value(c)
        return total

    for q in range(LOADS):
        gather(-res_ref[pl.ds(q * per, per), :], oh_r)
        load(q).wait()
        add_back(q * per, per, q == 0)
    pl.semaphore_wait(barrier, row.n + col.n - 2)
    spread(oh_c, sums[0])

    def p0(c):
        return full_r[0, c]

    for d in range(row.owners):
        c = sums[0].arrive(d)
        gather(p0(c), oh_c)
        if d == row.owners - 1:
            exchanges[0].start(pair(
                fold_all(row, lambda e: fold(p0(e) * p0(e))),
                fold_all(row, lambda e: fold(p0(e) * damp(e) * p0(e))),
            ))
        add_forth(c * row.rows, row.rows, d == 0)
    close_forth()
    spread(oh_r, sums[1])

    for d in range(col.owners):
        c = sums[1].arrive(d)
        gather(full_c[0, c], oh_r)
        if d == col.owners - 1:
            exchanges[1].start(pair(fold_all(col, lambda e: fold(full_c[0, e] * full_c[0, e]))))
        add_back(c * col.rows, col.rows, d == 0)
    spread(oh_c, sums[2])

    both = exchanges[0].total()
    norm0 = whole(both[:SUB])
    alpha0 = norm0 / (whole(exchanges[1].total()[:SUB]) + whole(both[SUB:]))

    for d in range(row.owners):
        c = sums[2].arrive(d)
        r1 = p0(c) - alpha0 * (full_r[1, c] + damp(c) * p0(c))
        r1_ref[c] = r1
        gather(r1, oh_c)
        if d == row.owners - 1:
            exchanges[2].start(pair(fold_all(row, lambda e: fold(r1_ref[e] * r1_ref[e]))))
        add_forth(c * row.rows, row.rows, d == 0)
    close_forth()
    spread(oh_r, sums[3])

    norm1 = whole(exchanges[2].total()[:SUB])
    beta = norm1 / norm0

    def p1(c):
        return r1_ref[c] + beta * p0(c)

    def image1(c):
        return full_c[1, c] + beta * full_c[0, c]

    exchanges[4].start(pair(fold_all(row, lambda e: fold(p1(e) * damp(e) * p1(e)))))
    for d in range(col.owners):
        c = sums[3].arrive(d)
        gather(image1(c), oh_r)
        if d == col.owners - 1:
            exchanges[3].start(pair(fold_all(col, lambda e: fold(image1(e) * image1(e)))))
        add_back(c * col.rows, col.rows, d == 0)
    spread(oh_c, sums[4])

    curv1 = whole(exchanges[3].total()[:SUB]) + whole(exchanges[4].total()[:SUB])
    alpha1 = norm1 / curv1
    for d in range(row.owners):
        c = sums[4].arrive(d)
        at = pl.ds(pl.multiple_of(c * row.rows, SUB), row.rows)
        step_ref[at, :] = alpha0 * p0(c) + alpha1 * p1(c)
        out_ref[at, :] = r1_ref[c] - alpha1 * (full_r[2, c] + damp(c) * p1(c))

    for s in sums:
        s.drain()
    for e in exchanges:
        e.drain()


def on_device(n_row, n_col, jacobian, block_rows, block_cols, counts, residuals, damping):
    entries, _, slots = jacobian.shape[2:]
    res_width = residuals.shape[1]
    par_width = damping.shape[1]
    row = Group("row", n_row, entries)
    col = Group("col", n_col, entries)
    n = max(n_row, n_col)
    own = max(row.owners, col.owners)
    vmem = pl.BlockSpec(memory_space=pltpu.VMEM)
    dma = pltpu.SemaphoreType.DMA
    out = jax.ShapeDtypeStruct((entries, par_width), F32)
    return pl.pallas_call(
        functools.partial(kernel, row, col),
        out_shape=(out, out),
        in_specs=[
            pl.BlockSpec(memory_space=pl.ANY),
            vmem,
            vmem,
            pl.BlockSpec(memory_space=pltpu.SMEM),
            vmem,
            vmem,
        ],
        out_specs=(vmem, vmem),
        scratch_shapes=[
            pltpu.VMEM((entries, entries, slots), BF16),
            pltpu.VMEM((res_width, slots), BF16),
            pltpu.VMEM((par_width, slots), BF16),
            pltpu.VMEM((max(row.rows, col.rows), slots), F32),
            pltpu.VMEM((entries, slots), F32),
            pltpu.VMEM((entries, SUB, slots), F32),
            pltpu.VMEM((row.owners, row.rows, par_width), F32),
            pltpu.VMEM((3, row.owners, row.rows, par_width), F32),
            pltpu.VMEM((3, n_row, row.rows, par_width), F32),
            pltpu.VMEM((3, row.owners, row.rows, par_width), F32),
            pltpu.VMEM((2, col.owners, col.rows, res_width), F32),
            pltpu.VMEM((2, n_col, col.rows, res_width), F32),
            pltpu.VMEM((2, col.owners, col.rows, res_width), F32),
            pltpu.VMEM((5, n, 2 * SUB, LANES), F32),
            dma((LOADS,)),
            dma((2, 3, own)),
            dma((2, 3, n)),
            dma((2, 3, n)),
            dma((2, 3, own)),
            dma((5, n)),
            dma((5, n)),
        ],
        compiler_params=pltpu.CompilerParams(
            collective_id=0, has_side_effects=True, vmem_limit_bytes=48 * 1024 * 1024
        ),
        cost_estimate=pl.CostEstimate(
            flops=10 * entries * entries * slots,
            bytes_accessed=2 * entries * entries * slots,
            transcendentals=0,
        ),
        name="cg",
    )(
        jacobian.reshape(entries, entries, slots),
        block_rows.reshape(1, slots),
        block_cols.reshape(1, slots),
        counts,
        residuals,
        damping,
    )


def solution(mesh):
    placed = (
        P(("rig", "row"), "col", None, None, None),
        P(("rig", "row"), "col", None),
        P(("rig", "row"), "col", None),
        P(("rig", "row"), "col"),
        P(None, ("rig", "row")),
        P(None, ("rig", "col")),
    )
    return jax.shard_map(
        functools.partial(on_device, mesh.shape["row"], mesh.shape["col"]),
        mesh=mesh,
        in_specs=placed,
        out_specs=(P(None, ("rig", "col")), P(None, ("rig", "col"))),
        check_vma=False,
    )
```

```python
import functools

import jax
import jax.numpy as jnp
from jax import lax
from jax.experimental import pallas as pl
from jax.experimental.pallas import tpu as pltpu
from jax.sharding import PartitionSpec as P

F32 = jnp.float32
BF16 = jnp.bfloat16
MESH = pl.DeviceIdType.MESH
LANES = 128
SUB = 8
LOADS = 4
HALVES = 2
PIECES = 2


class Group:
    def __init__(self, axis, size):
        self.axis, self.n = axis, size

    def locate(self):
        self.me = lax.axis_index(self.axis)

    def peer(self, d):
        return lax.rem(self.me + d, self.n)

    def remote(self, src, dst, send, recv, target):
        return pltpu.make_async_remote_copy(
            src_ref=src, dst_ref=dst, send_sem=send, recv_sem=recv,
            device_id={self.axis: target}, device_id_type=MESH,
        )


class LineSum:
    def __init__(self, group, k, part, recv, full, sems):
        self.g, self.k = group, k
        self.part, self.recv, self.full = part, recv, full
        self.rs_send, self.rs_recv, self.ag_send, self.ag_recv = sems
        self.base = group.n // 2 - 1
        self.near = jnp.where(group.me <= self.base, 0, 1)

    def piece(self, q):
        rows = self.part.shape[2] // PIECES
        return pl.ds(q * rows, rows)

    def rs(self, c, q, src, target):
        k, at = self.k, self.piece(q)
        return self.g.remote(
            self.part.at[k, c, at], self.recv.at[k, src, at],
            self.rs_send.at[k, c, q], self.rs_recv.at[k, src, q], target,
        )

    def ag(self, c, q, target):
        k, at = self.k, self.piece(q)
        return self.g.remote(
            self.full.at[k, c, at], self.full.at[k, c, at],
            self.ag_send.at[k, target, q], self.ag_recv.at[k, c, q], target,
        )

    def is_owner(self):
        return self.g.me == self.base + self.near

    def places(self):
        toward = 1 - 2 * self.near
        half = self.g.n // 2
        steps = list(range(half, 0, -1)) + [-e for e in range(half - 1, 0, -1)]
        return [self.g.me + toward * e for e in steps]

    def order(self):
        return (1 - self.near, self.near)

    def send(self, place):
        g, c = self.g, self.order()[place]

        def start():
            for q in range(PIECES):
                self.rs(c, q, g.me, self.base + c).start()

        if place == 0:
            start()
        else:
            pl.when(jnp.logical_not(self.is_owner()))(start)

    def reduce(self):
        @pl.when(self.is_owner())
        def _():
            for q in range(PIECES):
                at = self.piece(q)
                total = self.part[self.k, self.near, at, :]
                for src in reversed(self.places()):
                    self.rs(self.near, q, src, self.g.me).wait_recv()
                    total = total + self.recv[self.k, src, at, :]
                self.full[self.k, self.near, at, :] = total
                for target in self.places():
                    self.ag(self.near, q, target).start()

    def arrive(self, d):
        if d == 0:
            @pl.when(jnp.logical_not(self.is_owner()))
            def _():
                for q in range(PIECES):
                    self.ag(self.near, q, self.g.me).wait_recv()

            return self.near
        for q in range(PIECES):
            self.ag(1 - self.near, q, self.g.me).wait_recv()
        return 1 - self.near

    def drain(self):
        g, far = self.g, 1 - self.near
        for q in range(PIECES):
            self.rs(far, q, g.me, self.base + far).wait_send()

        @pl.when(jnp.logical_not(self.is_owner()))
        def _():
            for q in range(PIECES):
                self.rs(self.near, q, g.me, self.base + self.near).wait_send()

        @pl.when(self.is_owner())
        def _():
            for q in range(PIECES):
                for target in self.places():
                    self.ag(self.near, q, target).wait_send()


class PairSum:
    def __init__(self, group, k, part, recv, halves, full, sems):
        self.g, self.k = group, k
        self.part, self.recv, self.halves, self.full = part, recv, halves, full
        self.a_send, self.a_recv, self.x_send, self.x_recv, self.b_send, self.b_recv = sems
        self.h = lax.rem(group.me, 2)
        self.chip = group.me // 2
        self.chips = group.n // 2
        self.pair = group.me + 1 - 2 * self.h

    def first(self, c):
        k = self.k
        return self.g.remote(
            self.part.at[k, c], self.recv.at[k], self.a_send.at[k], self.a_recv.at[k], self.pair
        )

    def cross(self, slot, chip):
        k = self.k
        return self.g.remote(
            self.halves.at[k, slot], self.halves.at[k, slot],
            self.x_send.at[k, chip], self.x_recv.at[k, slot], 2 * chip + self.h,
        )

    def last(self, c):
        k = self.k
        return self.g.remote(
            self.full.at[k, c], self.full.at[k, c], self.b_send.at[k], self.b_recv.at[k], self.pair
        )

    def others(self):
        return [lax.rem(self.chip + e, self.chips) for e in range(1, self.chips)]

    def order(self):
        return (1 - self.h, self.h)

    def send(self, place):
        if place == 0:
            self.first(1 - self.h).start()

    def reduce(self):
        k = self.k
        self.first(self.h).wait_recv()
        self.halves[k, self.chip] = self.part[k, self.h] + self.recv[k]
        for chip in self.others():
            self.cross(self.chip, chip).start()
        for chip in self.others():
            self.cross(chip, chip).wait_recv()
        total = self.halves[k, 0]
        for slot in range(1, self.chips):
            total = total + self.halves[k, slot]
        self.full[k, self.h] = total
        self.last(self.h).start()

    def arrive(self, d):
        if d == 0:
            return self.h
        self.last(1 - self.h).wait_recv()
        return 1 - self.h

    def drain(self):
        self.first(1 - self.h).wait_send()
        for chip in self.others():
            self.cross(self.chip, chip).wait_send()
        self.last(self.h).wait_send()


class Tile:
    def __init__(self, group, k, buf, send, recv):
        self.g, self.k, self.buf, self.send, self.recv = group, k, buf, send, recv

    def copy(self, slot, target):
        return pltpu.make_async_remote_copy(
            src_ref=self.buf.at[self.k, slot],
            dst_ref=self.buf.at[self.k, slot],
            send_sem=self.send.at[self.k, target],
            recv_sem=self.recv.at[self.k, slot],
            device_id={self.g.axis: target},
            device_id_type=MESH,
        )

    def start(self, value):
        g = self.g
        self.buf[self.k, g.me] = value
        for d in range(1, g.n):
            self.copy(g.me, g.peer(d)).start()

    def total(self):
        g = self.g
        for d in range(1, g.n):
            self.copy(g.peer(d), g.me).wait_recv()
        total = self.buf[self.k, 0]
        for slot in range(1, g.n):
            total = total + self.buf[self.k, slot]
        return total

    def drain(self):
        for d in range(1, self.g.n):
            self.copy(self.g.me, self.g.peer(d)).wait_send()


def pieces(x):
    high = x.astype(BF16)
    low = (x - high.astype(F32)).astype(BF16)
    return jnp.concatenate([high, low], axis=0)


def fold(x):
    total = None
    for r in range(0, x.shape[0], SUB):
        for c in range(0, x.shape[1], LANES):
            block = x[r : r + SUB, c : c + LANES]
            total = block if total is None else total + block
    return total


def whole(tile):
    return jnp.sum(tile, axis=(0, 1), keepdims=True)


def kernel(
    row, col, jac_hbm, rows_hbm, cols_hbm, count_ref, res_hbm, damp_hbm, step_ref, out_ref,
    jac, rows_ref, cols_ref, res_ref, damp_ref, oh_r, oh_c, g_ref, terms, acc3, r1_ref,
    part_r, recv_r, full_r, part_c, recv_c, halves, full_c, tiles,
    load_sem, small_sem, rs_send, rs_recv, ag_send, ag_recv,
    a_send, a_recv, x_send, x_recv, b_send, b_recv, t_send, t_recv,
):
    entries, _, slots = jac.shape
    rows = entries // HALVES
    row.locate()
    col.locate()
    sems_r = (rs_send, rs_recv, ag_send, ag_recv)
    sems_c = (a_send, a_recv, x_send, x_recv, b_send, b_recv)

    barrier = pltpu.get_barrier_semaphore()
    for g in (row, col):
        for d in range(1, g.n):
            pl.semaphore_signal(
                barrier, inc=1, device_id={g.axis: g.peer(d)}, device_id_type=MESH
            )

    small = [
        pltpu.make_async_copy(src, dst, small_sem.at[q])
        for q, (src, dst) in enumerate((
            (rows_hbm, rows_ref), (cols_hbm, cols_ref), (res_hbm, res_ref), (damp_hbm, damp_ref),
        ))
    ]
    for copy in small:
        copy.start()
    per = entries // LOADS

    def load(q):
        part = pl.ds(q * per, per)
        return pltpu.make_async_copy(jac_hbm.at[part], jac.at[part], load_sem.at[q])

    for q in range(LOADS):
        load(q).start()
    for copy in small:
        copy.wait()

    live = lax.broadcasted_iota(jnp.int32, (1, slots), 1) < count_ref[0, 0]
    for idx_ref, oh in ((rows_ref, oh_r), (cols_ref, oh_c)):
        width = oh.shape[0]
        index = jnp.where(live, idx_ref[...], -1)
        step = 64

        def build(i, _, index=index, oh=oh, step=step):
            at = pl.multiple_of(i * step, step)
            ids = lax.broadcasted_iota(jnp.int32, (step, slots), 0) + at
            oh[pl.ds(at, step), :] = jnp.where(ids == index, 1.0, 0.0).astype(BF16)
            return 0

        lax.fori_loop(0, width // step, build, 0)

    def gather(x, oh):
        count = x.shape[0]
        y = jnp.dot(pieces(x), oh[...], preferred_element_type=F32)
        g_ref[pl.ds(0, count), :] = y[:count] + y[count:]

    def add_back(a0, count, first, half=None):
        width = entries if half is None else rows
        b0 = 0 if half is None else pl.multiple_of(half * rows, rows)

        def body(kk, _):
            sl = pl.ds(pl.multiple_of(kk * LANES, LANES), LANES)
            acc = None if first else terms[pl.ds(b0, width), sl]
            for a in range(count):
                term = jac[a0 + a, pl.ds(b0, width), sl].astype(F32) * g_ref[a : a + 1, sl]
                acc = term if acc is None else acc + term
            terms[pl.ds(b0, width), sl] = acc
            return 0

        lax.fori_loop(0, slots // LANES, body, 0)

    def add_forth(b0, count, first, half=None):
        width = entries if half is None else rows
        a0 = 0 if half is None else pl.multiple_of(half * rows, rows)
        b0 = pl.multiple_of(b0, count)

        def body(kk, _):
            sl = pl.ds(pl.multiple_of(kk * LANES, LANES), LANES)
            g = g_ref[pl.ds(0, count), sl]
            for a in range(width):
                m = jac[a0 + a, pl.ds(b0, count), sl].astype(F32) * g
                part = m[:SUB]
                for r in range(SUB, count, SUB):
                    part = part + m[r : r + SUB]
                acc3[a0 + a, :, sl] = part if first else acc3[a0 + a, :, sl] + part
            if half is not None:
                terms[pl.ds(a0, width), sl] = jnp.sum(acc3[pl.ds(a0, width), :, sl], axis=1)
            return 0

        lax.fori_loop(0, slots // LANES, body, 0)

    def finish(s, oh, work):
        for place, half in enumerate(s.order()):
            work(half)
            y = lax.dot_general(
                pieces(terms[pl.ds(pl.multiple_of(half * rows, rows), rows), :]), oh[...],
                (((1,), (1,)), ((), ())), preferred_element_type=F32,
            )
            s.part[s.k, half] = y[:rows] + y[rows:]
            s.send(place)
        s.reduce()

    def sum_r(k):
        return LineSum(row, k, part_r, recv_r, full_r, sems_r)

    def sum_c(k):
        return PairSum(col, k, part_c, recv_c, halves, full_c, sems_c)

    sums = [sum_r(0), sum_c(0), sum_r(1), sum_c(1), sum_r(2)]
    groups = (col, row, col, row, col)
    exchanges = [Tile(g, k, tiles, t_send, t_recv) for k, g in enumerate(groups)]
    nothing = jnp.zeros((SUB, LANES), F32)

    def pair(first, second=nothing):
        return jnp.concatenate([first, second], axis=0)

    def damp(c):
        return damp_ref[pl.ds(pl.multiple_of(c * rows, rows), rows), :]

    def fold_all(value):
        total = value(0)
        for c in range(1, HALVES):
            total = total + value(c)
        return total

    for q in range(LOADS):
        gather(-res_ref[pl.ds(q * per, per), :], oh_r)
        load(q).wait()
        if q < LOADS - 1:
            add_back(q * per, per, q == 0)
    pl.semaphore_wait(barrier, row.n + col.n - 2)
    finish(sums[0], oh_c, lambda half: add_back((LOADS - 1) * per, per, False, half))

    def p0(c):
        return full_r[0, c]

    for d in range(HALVES):
        c = sums[0].arrive(d)
        gather(p0(c), oh_c)
        if d == HALVES - 1:
            exchanges[0].start(pair(
                fold_all(lambda e: fold(p0(e) * p0(e))),
                fold_all(lambda e: fold(p0(e) * damp(e) * p0(e))),
            ))
        if d < HALVES - 1:
            add_forth(c * rows, rows, True)
    finish(sums[1], oh_r, lambda half: add_forth(c * rows, rows, False, half))

    for d in range(HALVES):
        c = sums[1].arrive(d)
        gather(full_c[0, c], oh_r)
        if d == HALVES - 1:
            exchanges[1].start(pair(fold_all(lambda e: fold(full_c[0, e] * full_c[0, e]))))
        if d < HALVES - 1:
            add_back(c * rows, rows, True)
    finish(sums[2], oh_c, lambda half: add_back(c * rows, rows, False, half))

    both = exchanges[0].total()
    norm0 = whole(both[:SUB])
    alpha0 = norm0 / (whole(exchanges[1].total()[:SUB]) + whole(both[SUB:]))

    for d in range(HALVES):
        c = sums[2].arrive(d)
        r1 = p0(c) - alpha0 * (full_r[1, c] + damp(c) * p0(c))
        r1_ref[c] = r1
        gather(r1, oh_c)
        if d == HALVES - 1:
            exchanges[2].start(pair(fold_all(lambda e: fold(r1_ref[e] * r1_ref[e]))))
        if d < HALVES - 1:
            add_forth(c * rows, rows, True)
    finish(sums[3], oh_r, lambda half: add_forth(c * rows, rows, False, half))

    norm1 = whole(exchanges[2].total()[:SUB])
    beta = norm1 / norm0

    def p1(c):
        return r1_ref[c] + beta * p0(c)

    def image1(c):
        return full_c[1, c] + beta * full_c[0, c]

    exchanges[4].start(pair(fold_all(lambda e: fold(p1(e) * damp(e) * p1(e)))))
    for d in range(HALVES):
        c = sums[3].arrive(d)
        gather(image1(c), oh_r)
        if d == HALVES - 1:
            exchanges[3].start(pair(fold_all(lambda e: fold(image1(e) * image1(e)))))
        if d < HALVES - 1:
            add_back(c * rows, rows, True)
    finish(sums[4], oh_c, lambda half: add_back(c * rows, rows, False, half))

    curv1 = whole(exchanges[3].total()[:SUB]) + whole(exchanges[4].total()[:SUB])
    alpha1 = norm1 / curv1
    for d in range(HALVES):
        c = sums[4].arrive(d)
        at = pl.ds(pl.multiple_of(c * rows, rows), rows)
        step_ref[at, :] = alpha0 * p0(c) + alpha1 * p1(c)
        out_ref[at, :] = r1_ref[c] - alpha1 * (full_r[2, c] + damp(c) * p1(c))

    for s in sums:
        s.drain()
    for e in exchanges:
        e.drain()


def on_device(n_row, n_col, jacobian, block_rows, block_cols, counts, residuals, damping):
    entries, _, slots = jacobian.shape[2:]
    res_width = residuals.shape[1]
    par_width = damping.shape[1]
    row = Group("row", n_row)
    col = Group("col", n_col)
    rows = entries // HALVES
    chips = n_col // 2
    n = max(n_row, n_col)
    vmem = pl.BlockSpec(memory_space=pltpu.VMEM)
    hbm = pl.BlockSpec(memory_space=pl.ANY)
    dma = pltpu.SemaphoreType.DMA
    out = jax.ShapeDtypeStruct((entries, par_width), F32)
    return pl.pallas_call(
        functools.partial(kernel, row, col),
        out_shape=(out, out),
        in_specs=[hbm, hbm, hbm, pl.BlockSpec(memory_space=pltpu.SMEM), hbm, hbm],
        out_specs=(vmem, vmem),
        scratch_shapes=[
            pltpu.VMEM((entries, entries, slots), BF16),
            pltpu.VMEM((1, slots), jnp.int32),
            pltpu.VMEM((1, slots), jnp.int32),
            pltpu.VMEM((entries, res_width), F32),
            pltpu.VMEM((entries, par_width), F32),
            pltpu.VMEM((res_width, slots), BF16),
            pltpu.VMEM((par_width, slots), BF16),
            pltpu.VMEM((rows, slots), F32),
            pltpu.VMEM((entries, slots), F32),
            pltpu.VMEM((entries, SUB, slots), F32),
            pltpu.VMEM((HALVES, rows, par_width), F32),
            pltpu.VMEM((3, HALVES, rows, par_width), F32),
            pltpu.VMEM((3, n_row, rows, par_width), F32),
            pltpu.VMEM((3, HALVES, rows, par_width), F32),
            pltpu.VMEM((2, HALVES, rows, res_width), F32),
            pltpu.VMEM((2, rows, res_width), F32),
            pltpu.VMEM((2, chips, rows, res_width), F32),
            pltpu.VMEM((2, HALVES, rows, res_width), F32),
            pltpu.VMEM((5, n, 2 * SUB, LANES), F32),
            dma((LOADS,)),
            dma((4,)),
            dma((3, HALVES, PIECES)),
            dma((3, n_row, PIECES)),
            dma((3, n_row, PIECES)),
            dma((3, HALVES, PIECES)),
            dma((2,)),
            dma((2,)),
            dma((2, chips)),
            dma((2, chips)),
            dma((2,)),
            dma((2,)),
            dma((5, n)),
            dma((5, n)),
        ],
        compiler_params=pltpu.CompilerParams(
            collective_id=0, has_side_effects=True, vmem_limit_bytes=48 * 1024 * 1024
        ),
        cost_estimate=pl.CostEstimate(
            flops=10 * entries * entries * slots,
            bytes_accessed=2 * entries * entries * slots,
            transcendentals=0,
        ),
        name="cg",
    )(
        jacobian.reshape(entries, entries, slots),
        block_rows.reshape(1, slots),
        block_cols.reshape(1, slots),
        counts,
        residuals,
        damping,
    )


def solution(mesh):
    placed = (
        P(("rig", "row"), "col", None, None, None),
        P(("rig", "row"), "col", None),
        P(("rig", "row"), "col", None),
        P(("rig", "row"), "col"),
        P(None, ("rig", "row")),
        P(None, ("rig", "col")),
    )
    return jax.shard_map(
        functools.partial(on_device, mesh.shape["row"], mesh.shape["col"]),
        mesh=mesh,
        in_specs=placed,
        out_specs=(P(None, ("rig", "col")), P(None, ("rig", "col"))),
        check_vma=False,
    )
```

```python
import functools

import jax
import jax.numpy as jnp
from jax import lax
from jax.experimental import pallas as pl
from jax.experimental.pallas import tpu as pltpu
from jax.sharding import PartitionSpec as P

F32 = jnp.float32
BF16 = jnp.bfloat16
MESH = pl.DeviceIdType.MESH
LANES = 128
SUB = 8
LOADS = 4
HALVES = 2
PIECES = 2


class Group:
    def __init__(self, axis, size):
        self.axis, self.n = axis, size

    def locate(self):
        self.me = lax.axis_index(self.axis)

    def peer(self, d):
        return lax.rem(self.me + d, self.n)

    def remote(self, src, dst, send, recv, target):
        return pltpu.make_async_remote_copy(
            src_ref=src, dst_ref=dst, send_sem=send, recv_sem=recv,
            device_id={self.axis: target}, device_id_type=MESH,
        )


class LineSum:
    def __init__(self, group, k, part, recv, full, sems):
        self.g, self.k = group, k
        self.part, self.recv, self.full = part, recv, full
        self.rs_send, self.rs_recv, self.ag_send, self.ag_recv = sems
        self.base = group.n // 2 - 1
        self.near = jnp.where(group.me <= self.base, 0, 1)

    def piece(self, q):
        rows = self.part.shape[2] // PIECES
        return pl.ds(q * rows, rows)

    def rs(self, c, q, src, target):
        k, at = self.k, self.piece(q)
        return self.g.remote(
            self.part.at[k, c, at], self.recv.at[k, src, at],
            self.rs_send.at[k, c, q], self.rs_recv.at[k, src, q], target,
        )

    def ag(self, c, q, target):
        k, at = self.k, self.piece(q)
        return self.g.remote(
            self.full.at[k, c, at], self.full.at[k, c, at],
            self.ag_send.at[k, target, q], self.ag_recv.at[k, c, q], target,
        )

    def is_owner(self):
        return self.g.me == self.base + self.near

    def places(self):
        toward = 1 - 2 * self.near
        half = self.g.n // 2
        steps = list(range(half, 0, -1)) + [-e for e in range(half - 1, 0, -1)]
        return [self.g.me + toward * e for e in steps]

    def order(self):
        return (1 - self.near, self.near)

    def send(self, place):
        g, c = self.g, self.order()[place]

        def start():
            for q in range(PIECES):
                self.rs(c, q, g.me, self.base + c).start()

        if place == 0:
            start()
        else:
            pl.when(jnp.logical_not(self.is_owner()))(start)

    def reduce(self):
        @pl.when(self.is_owner())
        def _():
            for q in range(PIECES):
                at = self.piece(q)
                total = self.part[self.k, self.near, at, :]
                for src in reversed(self.places()):
                    self.rs(self.near, q, src, self.g.me).wait_recv()
                    total = total + self.recv[self.k, src, at, :]
                self.full[self.k, self.near, at, :] = total
                for target in self.places():
                    self.ag(self.near, q, target).start()

    def arrive(self, d):
        if d == 0:
            @pl.when(jnp.logical_not(self.is_owner()))
            def _():
                for q in range(PIECES):
                    self.ag(self.near, q, self.g.me).wait_recv()

            return self.near
        for q in range(PIECES):
            self.ag(1 - self.near, q, self.g.me).wait_recv()
        return 1 - self.near

    def drain(self):
        g, far = self.g, 1 - self.near
        for q in range(PIECES):
            self.rs(far, q, g.me, self.base + far).wait_send()

        @pl.when(jnp.logical_not(self.is_owner()))
        def _():
            for q in range(PIECES):
                self.rs(self.near, q, g.me, self.base + self.near).wait_send()

        @pl.when(self.is_owner())
        def _():
            for q in range(PIECES):
                for target in self.places():
                    self.ag(self.near, q, target).wait_send()


class PairSum:
    def __init__(self, group, k, part, recv, halves, full, sems):
        self.g, self.k = group, k
        self.part, self.recv, self.halves, self.full = part, recv, halves, full
        self.a_send, self.a_recv, self.x_send, self.x_recv, self.b_send, self.b_recv = sems
        self.h = lax.rem(group.me, 2)
        self.chip = group.me // 2
        self.chips = group.n // 2
        self.pair = group.me + 1 - 2 * self.h

    def first(self, c):
        k = self.k
        return self.g.remote(
            self.part.at[k, c], self.recv.at[k], self.a_send.at[k], self.a_recv.at[k], self.pair
        )

    def cross(self, slot, chip):
        k = self.k
        return self.g.remote(
            self.halves.at[k, slot], self.halves.at[k, slot],
            self.x_send.at[k, chip], self.x_recv.at[k, slot], 2 * chip + self.h,
        )

    def last(self, c):
        k = self.k
        return self.g.remote(
            self.full.at[k, c], self.full.at[k, c], self.b_send.at[k], self.b_recv.at[k], self.pair
        )

    def others(self):
        return [lax.rem(self.chip + e, self.chips) for e in range(1, self.chips)]

    def order(self):
        return (1 - self.h, self.h)

    def send(self, place):
        if place == 0:
            self.first(1 - self.h).start()

    def reduce(self):
        k = self.k
        self.first(self.h).wait_recv()
        self.halves[k, self.chip] = self.part[k, self.h] + self.recv[k]
        for chip in self.others():
            self.cross(self.chip, chip).start()
        for chip in self.others():
            self.cross(chip, chip).wait_recv()
        total = self.halves[k, 0]
        for slot in range(1, self.chips):
            total = total + self.halves[k, slot]
        self.full[k, self.h] = total
        self.last(self.h).start()

    def arrive(self, d):
        if d == 0:
            return self.h
        self.last(1 - self.h).wait_recv()
        return 1 - self.h

    def drain(self):
        self.first(1 - self.h).wait_send()
        for chip in self.others():
            self.cross(self.chip, chip).wait_send()
        self.last(self.h).wait_send()


class Tile:
    def __init__(self, group, k, buf, send, recv):
        self.g, self.k, self.buf, self.send, self.recv = group, k, buf, send, recv

    def copy(self, slot, target):
        return pltpu.make_async_remote_copy(
            src_ref=self.buf.at[self.k, slot],
            dst_ref=self.buf.at[self.k, slot],
            send_sem=self.send.at[self.k, target],
            recv_sem=self.recv.at[self.k, slot],
            device_id={self.g.axis: target},
            device_id_type=MESH,
        )

    def start(self, value):
        g = self.g
        self.buf[self.k, g.me] = value
        for d in range(1, g.n):
            self.copy(g.me, g.peer(d)).start()

    def total(self):
        g = self.g
        for d in range(1, g.n):
            self.copy(g.peer(d), g.me).wait_recv()
        total = self.buf[self.k, 0]
        for slot in range(1, g.n):
            total = total + self.buf[self.k, slot]
        return total

    def drain(self):
        for d in range(1, self.g.n):
            self.copy(self.g.me, self.g.peer(d)).wait_send()


def pieces(x):
    high = x.astype(BF16)
    low = (x - high.astype(F32)).astype(BF16)
    return jnp.concatenate([high, low], axis=0)


def fold(x):
    total = None
    for r in range(0, x.shape[0], SUB):
        for c in range(0, x.shape[1], LANES):
            block = x[r : r + SUB, c : c + LANES]
            total = block if total is None else total + block
    return total


def whole(tile):
    return jnp.sum(tile, axis=(0, 1), keepdims=True)


def kernel(
    row, col, jac_hbm, rows_hbm, cols_hbm, count_ref, res_hbm, damp_hbm, step_ref, out_ref,
    jac, rows_ref, cols_ref, res_ref, damp_ref, oh_r, oh_c, g_ref, terms, acc3, r1_ref,
    part_r, recv_r, full_r, part_c, recv_c, halves, full_c, tiles,
    load_sem, small_sem, rs_send, rs_recv, ag_send, ag_recv,
    a_send, a_recv, x_send, x_recv, b_send, b_recv, t_send, t_recv,
):
    entries, _, slots = jac.shape
    rows = entries // HALVES
    row.locate()
    col.locate()
    sems_r = (rs_send, rs_recv, ag_send, ag_recv)
    sems_c = (a_send, a_recv, x_send, x_recv, b_send, b_recv)

    barrier = pltpu.get_barrier_semaphore()
    for g in (row, col):
        for d in range(1, g.n):
            pl.semaphore_signal(
                barrier, inc=1, device_id={g.axis: g.peer(d)}, device_id_type=MESH
            )

    small = [
        pltpu.make_async_copy(src, dst, small_sem.at[q])
        for q, (src, dst) in enumerate((
            (rows_hbm, rows_ref), (cols_hbm, cols_ref), (res_hbm, res_ref), (damp_hbm, damp_ref),
        ))
    ]
    for copy in small:
        copy.start()
    per = entries // LOADS

    def load(q):
        part = pl.ds(q * per, per)
        return pltpu.make_async_copy(jac_hbm.at[part], jac.at[part], load_sem.at[q])

    for q in range(LOADS):
        load(q).start()
    for copy in small:
        copy.wait()

    live = lax.broadcasted_iota(jnp.int32, (1, slots), 1) < count_ref[0, 0]
    for idx_ref, oh in ((rows_ref, oh_r), (cols_ref, oh_c)):
        width = oh.shape[0]
        index = jnp.where(live, idx_ref[...], -1)
        step = 64

        def build(i, _, index=index, oh=oh, step=step):
            at = pl.multiple_of(i * step, step)
            ids = lax.broadcasted_iota(jnp.int32, (step, slots), 0) + at
            oh[pl.ds(at, step), :] = jnp.where(ids == index, 1.0, 0.0).astype(BF16)
            return 0

        lax.fori_loop(0, width // step, build, 0)

    def gather(x, oh):
        count = x.shape[0]
        y = jnp.dot(pieces(x), oh[...], preferred_element_type=F32)
        g_ref[pl.ds(0, count), :] = y[:count] + y[count:]

    def add_back(a0, count, first, half=None):
        width = entries if half is None else rows
        b0 = 0 if half is None else pl.multiple_of(half * rows, rows)

        def body(kk, _):
            sl = pl.ds(pl.multiple_of(kk * LANES, LANES), LANES)
            acc = None if first else terms[pl.ds(b0, width), sl]
            for a in range(count):
                term = jac[a0 + a, pl.ds(b0, width), sl].astype(F32) * g_ref[a : a + 1, sl]
                acc = term if acc is None else acc + term
            terms[pl.ds(b0, width), sl] = acc
            return 0

        lax.fori_loop(0, slots // LANES, body, 0)

    def add_forth(b0, count, first, half=None):
        width = entries if half is None else rows
        a0 = 0 if half is None else pl.multiple_of(half * rows, rows)
        b0 = pl.multiple_of(b0, count)

        def body(kk, _):
            sl = pl.ds(pl.multiple_of(kk * LANES, LANES), LANES)
            g = g_ref[pl.ds(0, count), sl]
            sums_here = []
            for a in range(width):
                m = jac[a0 + a, pl.ds(b0, count), sl].astype(F32) * g
                part = m[:SUB]
                for r in range(SUB, count, SUB):
                    part = part + m[r : r + SUB]
                if not first:
                    part = part + acc3[a0 + a, :, sl]
                if half is None:
                    acc3[a0 + a, :, sl] = part
                    continue
                sums_here.append(part)
                if len(sums_here) == SUB:
                    at = pl.multiple_of(a0 + (a + 1 - SUB), SUB)
                    terms[pl.ds(at, SUB), sl] = jnp.sum(jnp.stack(sums_here), axis=1)
                    sums_here = []
            return 0

        lax.fori_loop(0, slots // LANES, body, 0)

    def finish(s, oh, work):
        for place, half in enumerate(s.order()):
            work(half)
            y = lax.dot_general(
                pieces(terms[pl.ds(pl.multiple_of(half * rows, rows), rows), :]), oh[...],
                (((1,), (1,)), ((), ())), preferred_element_type=F32,
            )
            s.part[s.k, half] = y[:rows] + y[rows:]
            s.send(place)
        s.reduce()

    def sum_r(k):
        return LineSum(row, k, part_r, recv_r, full_r, sems_r)

    def sum_c(k):
        return PairSum(col, k, part_c, recv_c, halves, full_c, sems_c)

    sums = [sum_r(0), sum_c(0), sum_r(1), sum_c(1), sum_r(2)]
    groups = (col, row, col, row, col)
    exchanges = [Tile(g, k, tiles, t_send, t_recv) for k, g in enumerate(groups)]
    nothing = jnp.zeros((SUB, LANES), F32)

    def pair(first, second=nothing):
        return jnp.concatenate([first, second], axis=0)

    def damp(c):
        return damp_ref[pl.ds(pl.multiple_of(c * rows, rows), rows), :]

    def fold_all(value):
        total = value(0)
        for c in range(1, HALVES):
            total = total + value(c)
        return total

    for q in range(LOADS):
        gather(-res_ref[pl.ds(q * per, per), :], oh_r)
        load(q).wait()
        if q < LOADS - 1:
            add_back(q * per, per, q == 0)
    pl.semaphore_wait(barrier, row.n + col.n - 2)
    finish(sums[0], oh_c, lambda half: add_back((LOADS - 1) * per, per, False, half))

    def p0(c):
        return full_r[0, c]

    for d in range(HALVES):
        c = sums[0].arrive(d)
        gather(p0(c), oh_c)
        if d == HALVES - 1:
            exchanges[0].start(pair(
                fold_all(lambda e: fold(p0(e) * p0(e))),
                fold_all(lambda e: fold(p0(e) * damp(e) * p0(e))),
            ))
        if d < HALVES - 1:
            add_forth(c * rows, rows, True)
    finish(sums[1], oh_r, lambda half: add_forth(c * rows, rows, False, half))

    for d in range(HALVES):
        c = sums[1].arrive(d)
        gather(full_c[0, c], oh_r)
        if d == HALVES - 1:
            exchanges[1].start(pair(fold_all(lambda e: fold(full_c[0, e] * full_c[0, e]))))
        if d < HALVES - 1:
            add_back(c * rows, rows, True)
    finish(sums[2], oh_c, lambda half: add_back(c * rows, rows, False, half))

    both = exchanges[0].total()
    norm0 = whole(both[:SUB])
    alpha0 = norm0 / (whole(exchanges[1].total()[:SUB]) + whole(both[SUB:]))

    for d in range(HALVES):
        c = sums[2].arrive(d)
        r1 = p0(c) - alpha0 * (full_r[1, c] + damp(c) * p0(c))
        r1_ref[c] = r1
        gather(r1, oh_c)
        if d == HALVES - 1:
            exchanges[2].start(pair(fold_all(lambda e: fold(r1_ref[e] * r1_ref[e]))))
        if d < HALVES - 1:
            add_forth(c * rows, rows, True)
    finish(sums[3], oh_r, lambda half: add_forth(c * rows, rows, False, half))

    norm1 = whole(exchanges[2].total()[:SUB])
    beta = norm1 / norm0

    def p1(c):
        return r1_ref[c] + beta * p0(c)

    def image1(c):
        return full_c[1, c] + beta * full_c[0, c]

    exchanges[4].start(pair(fold_all(lambda e: fold(p1(e) * damp(e) * p1(e)))))
    for d in range(HALVES):
        c = sums[3].arrive(d)
        gather(image1(c), oh_r)
        if d == HALVES - 1:
            exchanges[3].start(pair(fold_all(lambda e: fold(image1(e) * image1(e)))))
        if d < HALVES - 1:
            add_back(c * rows, rows, True)
    finish(sums[4], oh_c, lambda half: add_back(c * rows, rows, False, half))

    curv1 = whole(exchanges[3].total()[:SUB]) + whole(exchanges[4].total()[:SUB])
    alpha1 = norm1 / curv1
    for d in range(HALVES):
        c = sums[4].arrive(d)
        at = pl.ds(pl.multiple_of(c * rows, rows), rows)
        step_ref[at, :] = alpha0 * p0(c) + alpha1 * p1(c)
        out_ref[at, :] = r1_ref[c] - alpha1 * (full_r[2, c] + damp(c) * p1(c))

    for s in sums:
        s.drain()
    for e in exchanges:
        e.drain()


def on_device(n_row, n_col, jacobian, block_rows, block_cols, counts, residuals, damping):
    entries, _, slots = jacobian.shape[2:]
    res_width = residuals.shape[1]
    par_width = damping.shape[1]
    row = Group("row", n_row)
    col = Group("col", n_col)
    rows = entries // HALVES
    chips = n_col // 2
    n = max(n_row, n_col)
    vmem = pl.BlockSpec(memory_space=pltpu.VMEM)
    hbm = pl.BlockSpec(memory_space=pl.ANY)
    dma = pltpu.SemaphoreType.DMA
    out = jax.ShapeDtypeStruct((entries, par_width), F32)
    return pl.pallas_call(
        functools.partial(kernel, row, col),
        out_shape=(out, out),
        in_specs=[hbm, hbm, hbm, pl.BlockSpec(memory_space=pltpu.SMEM), hbm, hbm],
        out_specs=(vmem, vmem),
        scratch_shapes=[
            pltpu.VMEM((entries, entries, slots), BF16),
            pltpu.VMEM((1, slots), jnp.int32),
            pltpu.VMEM((1, slots), jnp.int32),
            pltpu.VMEM((entries, res_width), F32),
            pltpu.VMEM((entries, par_width), F32),
            pltpu.VMEM((res_width, slots), BF16),
            pltpu.VMEM((par_width, slots), BF16),
            pltpu.VMEM((rows, slots), F32),
            pltpu.VMEM((entries, slots), F32),
            pltpu.VMEM((entries, SUB, slots), F32),
            pltpu.VMEM((HALVES, rows, par_width), F32),
            pltpu.VMEM((3, HALVES, rows, par_width), F32),
            pltpu.VMEM((3, n_row, rows, par_width), F32),
            pltpu.VMEM((3, HALVES, rows, par_width), F32),
            pltpu.VMEM((2, HALVES, rows, res_width), F32),
            pltpu.VMEM((2, rows, res_width), F32),
            pltpu.VMEM((2, chips, rows, res_width), F32),
            pltpu.VMEM((2, HALVES, rows, res_width), F32),
            pltpu.VMEM((5, n, 2 * SUB, LANES), F32),
            dma((LOADS,)),
            dma((4,)),
            dma((3, HALVES, PIECES)),
            dma((3, n_row, PIECES)),
            dma((3, n_row, PIECES)),
            dma((3, HALVES, PIECES)),
            dma((2,)),
            dma((2,)),
            dma((2, chips)),
            dma((2, chips)),
            dma((2,)),
            dma((2,)),
            dma((5, n)),
            dma((5, n)),
        ],
        compiler_params=pltpu.CompilerParams(
            collective_id=0, has_side_effects=True, vmem_limit_bytes=48 * 1024 * 1024
        ),
        cost_estimate=pl.CostEstimate(
            flops=10 * entries * entries * slots,
            bytes_accessed=2 * entries * entries * slots,
            transcendentals=0,
        ),
        name="cg",
    )(
        jacobian.reshape(entries, entries, slots),
        block_rows.reshape(1, slots),
        block_cols.reshape(1, slots),
        counts,
        residuals,
        damping,
    )


def solution(mesh):
    placed = (
        P(("rig", "row"), "col", None, None, None),
        P(("rig", "row"), "col", None),
        P(("rig", "row"), "col", None),
        P(("rig", "row"), "col"),
        P(None, ("rig", "row")),
        P(None, ("rig", "col")),
    )
    return jax.shard_map(
        functools.partial(on_device, mesh.shape["row"], mesh.shape["col"]),
        mesh=mesh,
        in_specs=placed,
        out_specs=(P(None, ("rig", "col")), P(None, ("rig", "col"))),
        check_vma=False,
    )
```
